32 devices in a mesh: expert: 4 (over y, x), shard: 8 (over z, core).
Axes of the slice: x: 2, y: 2, z: 4, core: 2. Of those that a mesh axis runs over, the one named last changes fastest.
Arguments:
- tokens_in: bfloat16 [64, 128, 1024], P(('expert', 'shard')), may hold values from -6 to 6
- cotangent: bfloat16 [64, 128, 1024], P(('expert', 'shard')), may hold values from -6 to 6
- seq_lengths: int32 [64], P(('expert', 'shard')), may hold values from 64 to 128, as said below
- deal_perm: int32 [64], P(('expert', 'shard')), may hold values from 0 to 7, as said below
- routes: int32 [8192, 8], P(('expert', 'shard')), may hold values from 0 to 31, all different within a row; in each aligned block of 256 rows (0 to 255, 256 to 511, ...) at most 96 rows name the same one
- gate_logits: float32 [8192, 8], P(('expert', 'shard')), may hold values from -3 to 3
- first_gain: bfloat16 [1024], P('shard'), may hold values from 0.25 to 1.75
- query_weight: bfloat16 [1024, 1024], P('shard'), may hold values from -0.1875 to 0.1875
- key_matrix: bfloat16 [1024, 512], P('shard'), may hold values from -0.1875 to 0.1875
- value_matrix: bfloat16 [1024, 512], P('shard'), may hold values from -0.1875 to 0.1875
- output_weight: bfloat16 [1024, 1024], P('shard'), may hold values from -0.5 to 0.5
- second_gain: bfloat16 [1024], P('shard'), may hold values from 0.25 to 1.75
- gate_weight: bfloat16 [32, 1024, 512], P('expert', 'shard'), may hold values from -0.1875 to 0.1875
- up_weight: bfloat16 [32, 1024, 512], P('expert', 'shard'), may hold values from -0.1875 to 0.1875
- down_weight: bfloat16 [32, 512, 1024], P('expert', 'shard'), may hold values from -0.75 to 0.75
Outputs:
- layer_out: bfloat16 [64, 128, 1024], P(('expert', 'shard'))
- input_grad: bfloat16 [64, 128, 1024], P(('expert', 'shard'))
- first_gain_grad: float32 [1024], P('shard')
- query_grad: float32 [1024, 1024], P('shard')
- key_grad: float32 [1024, 512], P('shard')
- value_grad: float32 [1024, 512], P('shard')
- output_grad: float32 [1024, 1024], P('shard')
- second_gain_grad: float32 [1024], P('shard')
- gate_grad: float32 [32, 1024, 512], P('expert', 'shard')
- up_grad: float32 [32, 1024, 512], P('expert', 'shard')
- down_grad: float32 [32, 512, 1024], P('expert', 'shard')
The draws below stay inside these ranges and needn't reach their ends.
Inputs may be any that keep to these rules, and one draw needn't show every extreme that they name: seq_lengths[j] is the length of the sequence in dealt slot j; rows at or past it are padding. The lengths of one device's 2 slots sum to 192. Among the slots of the devices that share an index of shard, deal_perm is a permutation of those devices' given sequences, numbered as expert index times 2 plus slot. No two sequences go from one device to one device. `routes`: each row names 8 different experts. Within the rows of one device no expert is named by more than 96 rows, and in every draw some expert is named by exactly 96 rows of some device.
All inputs are finite; a program needn't handle non-finite values.
Results may differ from the reference program's by a relative error of at most 0.02.
Values may be sent and summed in bfloat16 or wider, within the bound.
No kernel may reach another device: no remote copies, remote signals or barrier semaphores. Data moves between devices by JAX's collectives and lax.ppermute only.
A program may use at most 192 MiB of HBM per device.

```python
import math
import jax
import jax.numpy as jnp
import numpy as np
from jax import lax

MODEL_WIDTH = 1024
QUERY_HEADS = 16
KEY_VALUE_HEADS = 8
HEAD_SIZE = 64
FF = 512
EXPERTS = 32
TOP = 8
SLOT_ROWS = 128
DEVICE_SEQUENCES = 2
DEVICE_ROWS = 256
SEQS = 64
TOKENS = 8192
GROUP_SEQS = 8
CAP = 96
N_SHARD = 8


def draw_seq_lengths(key, part):
    key = jax.random.fold_in(key, 11)
    first_key, second_key = jax.random.split(key)
    devices = SEQS // DEVICE_SEQUENCES
    leading = jax.random.randint(first_key, (devices,), SLOT_ROWS // 2, SLOT_ROWS + 1)
    longest = jax.random.randint(second_key, (), 0, devices)
    leading = jnp.where(jnp.arange(devices) == longest, SLOT_ROWS, leading)
    trailing = SLOT_ROWS + SLOT_ROWS // 2 - leading
    return jnp.stack([leading, trailing], axis=1).reshape(-1).astype(jnp.int32)


def draw_deal_perm(key, part):
    key = jax.random.fold_in(key, 23)
    order_key, offset_key = jax.random.split(key)
    members = GROUP_SEQS // DEVICE_SEQUENCES
    query_groups = SEQS // GROUP_SEQS
    group_keys = jax.random.split(order_key, query_groups)

    def shuffled(one_key):
        return jax.random.permutation(one_key, members)
    first = jax.vmap(shuffled)(group_keys).astype(jnp.int32)
    offset = jax.random.randint(offset_key, (query_groups, 1), 1, members).astype(jnp.int32)
    second = (first - offset) % members
    table = jnp.stack([first * DEVICE_SEQUENCES, second * DEVICE_SEQUENCES + 1], axis=-1)
    return jnp.transpose(table, (1, 0, 2)).reshape(-1).astype(jnp.int32)


def shard_levels(stream_key, dims, cuts, least, largest):
    gain, own = 1.0, jax.random.fold_in(stream_key, 6)
    for axis_at, parts in cuts:
        heights = jnp.exp(jax.random.uniform(jax.random.fold_in(own, axis_at), (parts,), jnp.float32, least / len(cuts), largest / len(cuts)))
        gain = gain * jnp.repeat(heights, dims[axis_at] // parts).reshape([-1 if axis == axis_at else 1 for axis in range(len(dims))])
    return gain


def deal_out(own_key, own, number, rows, amount, top, limit, slope):
    sequence = jax.random.permutation(own_key, amount)
    heavy_load, usual = portions_of(amount, rows * top, limit, slope, True), portions_of(amount, rows * top, limit, slope, False)
    places = jnp.arange(amount)

    def named(tallies, offset_by):
        used = int((tallies > 0).sum())
        fixed = max(1, used // 4)
        shifted = fixed + (places - fixed + offset_by * (used - fixed)) % max(1, amount - fixed)
        return jnp.zeros((amount,), jnp.int32).at[sequence[jnp.where(places < fixed, places, shifted)]].set(jnp.asarray(tallies, jnp.int32))

    tallies = jnp.where(number % 4 == 0, named(heavy_load, number // 4), named(usual, number - number // 4 - 1))
    mixed = jax.random.permutation(jax.random.fold_in(own, 3), amount)
    donor, sink = mixed[0:amount // 2 * 2:2], mixed[1:amount // 2 * 2:2]
    margin = jnp.minimum(tallies[donor] - 1, limit - tallies[sink]) // 2
    margin = jnp.where((donor == sequence[0]) | (sink == sequence[0]) | (tallies[sink] == 0), 0, jnp.maximum(margin, 0))
    shifted = jax.random.randint(jax.random.fold_in(own, 4), (amount // 2,), 0, 1 << 20) % (margin + 1)
    tallies = tallies.at[donor].add(-shifted).at[sink].add(shifted)
    items = jnp.searchsorted(jnp.cumsum(tallies), jnp.arange(rows * top), side="right").astype(jnp.int32)
    table = items.reshape(top, rows).T
    table = table[jax.random.permutation(jax.random.fold_in(own, 1), rows)]
    offset_by = jax.random.randint(jax.random.fold_in(own, 2), (rows, 1), 0, top)
    return jnp.take_along_axis(table, (jnp.arange(top)[None, :] + offset_by) % top, axis=1)


def portions_of(number_of, total, reach, lean, full):
    loads = [(1 << 20) // math.isqrt(grade ** lean) + 1 for grade in range(1, number_of + 1)]
    largest = reach if full else min(reach, max(-(-total // number_of), total * loads[0] // sum(loads)))
    least = 1 if total - largest >= number_of - 1 else 0
    given, rest = [largest] + [least] * (number_of - 1), total - largest - least * (number_of - 1)
    while rest > 0:
        movable = [i for i in range(1, number_of) if given[i] < largest] or [i for i in range(1, number_of) if given[i] < reach]
        whole, budget = sum([loads[i] for i in movable]), rest
        for i in movable:
            extra = min(reach - given[i], max(1, budget * loads[i] // whole), rest)
            given[i] = given[i] + extra
            rest = rest - extra
    return np.array(given)


def gaussian(rng, shape, deviation, reach, cuts=(), kind=jnp.bfloat16):
    level = shard_levels(rng, shape, cuts, -0.22, 0.18) if cuts else 1.0
    values = jax.random.normal(rng, shape, jnp.float32) * deviation * level
    return jnp.minimum(jnp.maximum(values, -reach), reach).astype(kind)


def setup_inputs(seed: int = 0) -> dict:
    key_of = jax.random.split(jax.random.key(seed), 16)
    tokens_in = gaussian(key_of[0], (SEQS, SLOT_ROWS, MODEL_WIDTH), 1.0, 6.0, ((0, 32),))
    cotangent = gaussian(key_of[1], (SEQS, SLOT_ROWS, MODEL_WIDTH), 1.0, 6.0, ((0, 32),))
    seq_lengths = draw_seq_lengths(jax.random.fold_in(key_of[15], 71), 0)
    deal_perm = draw_deal_perm(jax.random.fold_in(key_of[15], 71), 0)
    routes_keys = jax.random.split(jax.random.fold_in(key_of[4], 1), TOKENS // DEVICE_ROWS)
    routes_turns = jax.random.permutation(jax.random.fold_in(key_of[4], 3), TOKENS // DEVICE_ROWS)
    routes = jax.vmap(lambda own, number: deal_out(jax.random.fold_in(key_of[4], 2), own, number, DEVICE_ROWS, EXPERTS, TOP, CAP, 1))(routes_keys, routes_turns).reshape((TOKENS, TOP))
    gate_logits = gaussian(key_of[5], (TOKENS, TOP), 0.5, 3.0, ((0, 32),), jnp.float32)
    first_gain = jnp.clip(1.0 + 0.15 * jax.random.normal(key_of[6], (MODEL_WIDTH,), jnp.float32), 0.25, 1.75).astype(jnp.bfloat16)
    query_weight = gaussian(key_of[7], (MODEL_WIDTH, QUERY_HEADS * HEAD_SIZE), MODEL_WIDTH ** -0.5, 0.1875, ((0, 8),))
    key_matrix = gaussian(key_of[8], (MODEL_WIDTH, KEY_VALUE_HEADS * HEAD_SIZE), MODEL_WIDTH ** -0.5, 0.1875, ((0, 8),))
    value_matrix = gaussian(key_of[9], (MODEL_WIDTH, KEY_VALUE_HEADS * HEAD_SIZE), MODEL_WIDTH ** -0.5, 0.1875, ((0, 8),))
    output_weight = gaussian(key_of[10], (QUERY_HEADS * HEAD_SIZE, MODEL_WIDTH), (QUERY_HEADS * HEAD_SIZE // 8) ** -0.5, 0.5, ((0, 8),))
    second_gain = jnp.clip(1.0 + 0.15 * jax.random.normal(key_of[11], (MODEL_WIDTH,), jnp.float32), 0.25, 1.75).astype(jnp.bfloat16)
    gate_weight = gaussian(key_of[12], (EXPERTS, MODEL_WIDTH, FF), MODEL_WIDTH ** -0.5, 0.1875, ((0, 4), (1, 8)))
    up_weight = gaussian(key_of[13], (EXPERTS, MODEL_WIDTH, FF), MODEL_WIDTH ** -0.5, 0.1875, ((0, 4), (1, 8)))
    down_weight = gaussian(key_of[14], (EXPERTS, FF, MODEL_WIDTH), (FF // 8) ** -0.5, 0.75, ((0, 4), (1, 8)))
    return {"tokens_in": tokens_in, "cotangent": cotangent, "seq_lengths": seq_lengths, "deal_perm": deal_perm, "routes": routes, "gate_logits": gate_logits, "first_gain": first_gain, "query_weight": query_weight, "key_matrix": key_matrix, "value_matrix": value_matrix, "output_weight": output_weight, "second_gain": second_gain, "gate_weight": gate_weight, "up_weight": up_weight, "down_weight": down_weight}


epsilon = 1e-06
precise = lax.Precision.HIGHEST

@jax.custom_vjp
def lower_part(v):
    return lax.optimization_barrier(v.astype(jnp.bfloat16)).astype(jnp.float32)

@jax.custom_vjp
def low_back(v):
    return v

def low_keep(v):
    return (lower_part(v), None)

def low_pass(kept, grad):
    return (grad,)

def back_keep(v):
    return (v, None)

def back_low(kept, grad):
    return (lower_part(grad),)
lower_part.defvjp(low_keep, low_pass)
low_back.defvjp(back_keep, back_low)

def apply_rotation(field, sign):
    half = field.shape[-1] // 2
    position = jnp.arange(field.shape[-3], dtype=jnp.float32)
    frequency = 10000.0 ** (-jnp.arange(half, dtype=jnp.float32) * 2.0 / field.shape[-1])
    angles = position[:, None] * frequency[None, :]
    cosine_table = jnp.cos(angles)[:, None, :]
    sine_table = jnp.sin(angles)[:, None, :]
    first_half = field[..., :half]
    second_half = field[..., half:]
    return jnp.concatenate([first_half * cosine_table - sign * second_half * sine_table, second_half * cosine_table + sign * first_half * sine_table], axis=-1)

def layer_block(block_rows, lengths_here, routes_here, gates_here, params):
    first_gain, query_weight, key_matrix, value_matrix, output_weight, second_gain, gate_weight, up_weight, down_weight = params
    row_count = block_rows.shape[0]
    sequence_slots = lengths_here.shape[0]
    width = block_rows.shape[1]
    query_groups = QUERY_HEADS // KEY_VALUE_HEADS
    scale = HEAD_SIZE ** (-0.5)
    norm_one = lax.rsqrt(lax.optimization_barrier(jnp.mean(block_rows * block_rows, axis=-1, keepdims=True)) + epsilon)
    normed = lower_part(block_rows * norm_one * first_gain)
    query_unrotated = low_back(jnp.dot(normed, query_weight, precision=precise))
    key_unrotated = low_back(jnp.dot(normed, key_matrix, precision=precise))
    value_unrotated = low_back(jnp.dot(normed, value_matrix, precision=precise))
    query_rows = lower_part(apply_rotation(query_unrotated.reshape(sequence_slots, SLOT_ROWS, QUERY_HEADS, HEAD_SIZE), 1.0)).reshape(sequence_slots, SLOT_ROWS, KEY_VALUE_HEADS, query_groups, HEAD_SIZE)
    rotated_keys = lower_part(apply_rotation(key_unrotated.reshape(sequence_slots, SLOT_ROWS, KEY_VALUE_HEADS, HEAD_SIZE), 1.0))
    incoming_values = lower_part(value_unrotated.reshape(sequence_slots, SLOT_ROWS, KEY_VALUE_HEADS, HEAD_SIZE))
    raw_scores = jnp.einsum('bqgrd,bkgd->bgrqk', query_rows, rotated_keys, precision=precise)
    scores = low_back(raw_scores * scale)
    position = jnp.arange(SLOT_ROWS, dtype=jnp.int32)
    causal = (position[None, :] <= position[:, None])[None]
    live = position[None, None, :] < lengths_here[:, None, None]
    allowed = (causal & live)[:, None, None]
    masked = jnp.where(allowed, scores, -1e+30)
    probs = jax.nn.softmax(masked, axis=-1)
    mixed = lower_part(low_back(jnp.einsum('bgrqk,bkgd->bqgrd', lower_part(probs), incoming_values, precision=precise)))
    attended = low_back(jnp.dot(mixed.reshape(row_count, QUERY_HEADS * HEAD_SIZE), output_weight, precision=precise))
    after_attention = block_rows + attended
    norm_two = lax.rsqrt(lax.optimization_barrier(jnp.mean(after_attention * after_attention, axis=-1, keepdims=True)) + epsilon)
    routed_in = lower_part(after_attention * norm_two * second_gain)
    flat_experts = routes_here.reshape(-1)
    entries = flat_experts.shape[0]
    one_hot = (flat_experts[:, None] == jnp.arange(EXPERTS, dtype=jnp.int32)[None, :]).astype(jnp.int32)
    earlier = jnp.cumsum(one_hot, axis=0, dtype=jnp.int32) - one_hot
    target = (flat_experts * CAP + lax.optimization_barrier(jnp.sum(earlier * one_hot, axis=1, dtype=jnp.int32))).astype(jnp.int32)
    source_row = jnp.zeros((EXPERTS * CAP,), jnp.int32).at[target].set(jnp.arange(entries, dtype=jnp.int32))
    occupied = jnp.zeros((EXPERTS * CAP,), jnp.float32).at[target].set(1.0)
    expert_rows = low_back(routed_in[source_row // TOP] * occupied[:, None]).reshape(EXPERTS, CAP, width)
    gate_act = low_back(jnp.einsum('xcd,xdf->xcf', expert_rows, gate_weight, precision=precise))
    up_act = low_back(jnp.einsum('xcd,xdf->xcf', expert_rows, up_weight, precision=precise))
    hidden = lower_part(jax.nn.silu(gate_act) * up_act)
    expert_out = lower_part(low_back(jnp.einsum('xcf,xfd->xcd', hidden, down_weight, precision=precise)))
    returned = expert_out.reshape(EXPERTS * CAP, width)[target].reshape(row_count, TOP, width)
    weights = jax.nn.softmax(gates_here, axis=-1)
    combined = lax.optimization_barrier(jnp.sum(weights[:, :, None] * returned, axis=1))
    return after_attention + combined

def reference(tokens_in, cotangent, seq_lengths, deal_perm, routes, gate_logits, first_gain, query_weight, key_matrix, value_matrix, output_weight, second_gain, gate_weight, up_weight, down_weight):
    slot_index = jnp.arange(SEQS, dtype=jnp.int32)
    shard_place = slot_index // DEVICE_SEQUENCES % N_SHARD
    source = ((deal_perm // DEVICE_SEQUENCES * N_SHARD + shard_place) * DEVICE_SEQUENCES + deal_perm % DEVICE_SEQUENCES).astype(jnp.int32)
    inverse = jnp.argsort(source).astype(jnp.int32)
    devices = SEQS // DEVICE_SEQUENCES
    lengths_blocks = seq_lengths.reshape(devices, DEVICE_SEQUENCES)
    routes_blocks = routes.reshape(devices, DEVICE_ROWS, TOP)
    gates_blocks = gate_logits.astype(jnp.float32).reshape(devices, DEVICE_ROWS, TOP)

    def forward(token_rows, *params):
        dealt = token_rows[source].reshape(devices, DEVICE_ROWS, MODEL_WIDTH)

        def one_block(pieces):
            return layer_block(pieces[0], pieces[1], pieces[2], pieces[3], params)
        results = lax.map(jax.checkpoint(one_block), (dealt, lengths_blocks, routes_blocks, gates_blocks))
        return results.reshape(SEQS, SLOT_ROWS, MODEL_WIDTH)[inverse]
    weight_args = (first_gain, query_weight, key_matrix, value_matrix, output_weight, second_gain, gate_weight, up_weight, down_weight)
    floats = tuple((weight_arg.astype(jnp.float32) for weight_arg in weight_args))
    layer_out, pull_back = jax.vjp(forward, tokens_in.astype(jnp.float32), *floats)
    grads = pull_back(cotangent.astype(jnp.float32))
    return (layer_out.astype(jnp.bfloat16), grads[0].astype(jnp.bfloat16), grads[1], grads[2], grads[3], grads[4], grads[5], grads[6], grads[7], grads[8], grads[9])
```

```python
import functools

import jax
import jax.numpy as jnp
from jax import lax
from jax.experimental import pallas as pl
from jax.experimental.pallas import tpu as pltpu
from jax.sharding import PartitionSpec as P

WIDTH = 1024
HEADS = 16
KV_HEADS = 8
HEAD = 64
FF = 512
EXPERTS = 32
TOP = 8
SLOT = 128
SEQUENCES = 2
ROWS = 256
MOST = 192
PAD = 16
EPS = 1e-06
BF = jnp.bfloat16
F32 = jnp.float32
MIB = 1024 * 1024
ANY = pl.BlockSpec(memory_space=pl.ANY)
VM = pl.BlockSpec(memory_space=pltpu.VMEM)
SM = pl.BlockSpec(memory_space=pltpu.SMEM)


def window_of(n_shard):
    window = 112 if n_shard <= 8 else 64
    return window, -(-MOST // window)


def nn(a, b):
    return lax.dot_general(a, b, (((1,), (0,)), ((), ())), preferred_element_type=F32)


def nt(a, b):
    return lax.dot_general(a, b, (((1,), (1,)), ((), ())), preferred_element_type=F32)


def tn(a, b):
    return lax.dot_general(a, b, (((0,), (0,)), ((), ())), preferred_element_type=F32)


def cost(flops, traffic):
    return pl.CostEstimate(flops=int(flops), bytes_accessed=int(traffic), transcendentals=0)


def params(limit):
    return pltpu.CompilerParams(vmem_limit_bytes=limit * MIB)


def rotation_tables():
    half = HEAD // 2
    position = jnp.arange(SLOT, dtype=F32)
    frequency = 10000.0 ** (-jnp.arange(half, dtype=F32) * 2.0 / HEAD)
    angles = position[:, None] * frequency[None, :]
    cosine, sine = jnp.cos(angles), jnp.sin(angles)
    return (
        jnp.concatenate([cosine] * 4, axis=1),
        jnp.concatenate([-sine, sine] * 2, axis=1),
    )


def turn(field, cosine, sine, sign):
    lanes = lax.broadcasted_iota(jnp.int32, (SEQUENCES * SLOT, 128), 1)
    first = lanes % HEAD < HEAD // 2
    cosine = jnp.concatenate([cosine] * SEQUENCES, axis=0)
    sine = jnp.concatenate([sine] * SEQUENCES, axis=0) * sign
    parts = []
    for at in range(0, field.shape[1], 128):
        part = field[:, at : at + 128]
        other = jnp.where(
            first, pltpu.roll(part, 128 - HEAD // 2, 1), pltpu.roll(part, HEAD // 2, 1)
        )
        parts.append(part * cosine + other * sine)
    return jnp.concatenate(parts, axis=1)


def attention_kernel(
    ds, x_ref, pack_ref, gain_ref, cos_ref, sin_ref, len_ref,
    normed_ref, q_ref, kv_ref, probs_ref, mixed_ref, after_ref, routed_ref,
):
    x = x_ref[...].astype(F32)
    r1 = lax.rsqrt(jnp.mean(x * x, axis=-1, keepdims=True) + EPS)
    normed = (x * r1 * gain_ref[0:1, :]).astype(BF)
    normed_ref[...] = normed
    cosine, sine = cos_ref[...], sin_ref[...]
    q_raw = nn(normed, pack_ref[:, 0:ds, :].reshape(WIDTH, WIDTH))
    kv_raw = nn(normed, pack_ref[:, 2 * ds : 3 * ds, :].reshape(WIDTH, WIDTH))
    q_ref[...] = turn(q_raw, cosine, sine, 1.0).astype(BF)
    kv_ref[:, 0:FF] = turn(kv_raw[:, 0:FF], cosine, sine, 1.0).astype(BF)
    kv_ref[:, FF:] = kv_raw[:, FF:].astype(BF)
    row = lax.broadcasted_iota(jnp.int32, (2 * SLOT, SLOT), 0) % SLOT
    col = lax.broadcasted_iota(jnp.int32, (2 * SLOT, SLOT), 1)
    for b in range(SEQUENCES):
        allowed = (col <= row) & (col < len_ref[b])
        rows = slice(b * SLOT, (b + 1) * SLOT)
        for g in range(KV_HEADS):
            at = 2 * HEAD * g
            q2 = jnp.concatenate(
                [q_ref[rows, at : at + HEAD], q_ref[rows, at + HEAD : at + 2 * HEAD]], axis=0
            )
            keys = kv_ref[rows, HEAD * g : HEAD * (g + 1)]
            values = kv_ref[rows, FF + HEAD * g : FF + HEAD * (g + 1)]
            scores = jnp.where(allowed, nt(q2, keys) * HEAD**-0.5, -1e30)
            lifted = jnp.exp(scores - jnp.max(scores, axis=-1, keepdims=True))
            probs = lifted / jnp.sum(lifted, axis=-1, keepdims=True)
            probs_ref[b, g] = probs
            out = nn(probs.astype(BF), values).astype(BF)
            mixed_ref[rows, at : at + 2 * HEAD] = jnp.concatenate([out[:SLOT], out[SLOT:]], axis=1)
    after = x + nn(mixed_ref[...], pack_ref[:, ds : 2 * ds, :].reshape(WIDTH, WIDTH))
    after_ref[...] = after
    r2 = lax.rsqrt(jnp.mean(after * after, axis=-1, keepdims=True) + EPS)
    routed_ref[...] = (after * r2 * gain_ref[1:2, :]).astype(BF)


def attention_forward(ds, x, pack, gains, cosine, sine, lengths):
    shapes = [
        ((ROWS, WIDTH), BF),
        ((ROWS, WIDTH), BF),
        ((ROWS, WIDTH), BF),
        ((SEQUENCES, KV_HEADS, 2 * SLOT, SLOT), F32),
        ((ROWS, WIDTH), BF),
        ((ROWS, WIDTH), F32),
        ((ROWS, WIDTH), BF),
    ]
    return pl.pallas_call(
        functools.partial(attention_kernel, ds),
        out_shape=[jax.ShapeDtypeStruct(s, d) for s, d in shapes],
        in_specs=[VM] * 5 + [SM],
        out_specs=[VM] * 7,
        compiler_params=params(48),
        cost_estimate=cost(2e9, 12 * MIB),
        name="attention_forward",
    )(x, pack, gains, cosine, sine, lengths)


def attention_back_kernel(
    ds, n_shard, x_ref, cot_ref, after_ref, sum_ref, normed_ref, q_ref, kv_ref, probs_ref,
    mixed_ref, pack_ref, gain_ref, cos_ref, sin_ref,
    grad_ref, pieces_ref, dq_ref, dkv_ref,
):
    x, after = x_ref[...].astype(F32), after_ref[...]
    routed_grad = sum_ref[...].astype(F32)
    r2 = lax.rsqrt(jnp.mean(after * after, axis=-1, keepdims=True) + EPS)
    gain_two = jnp.sum(routed_grad * after * r2, axis=0, keepdims=True)
    scaled = routed_grad * gain_ref[1:2, :]
    residual = (
        cot_ref[...].astype(F32)
        + r2 * scaled
        - after * (r2 * r2 * r2) * jnp.mean(scaled * after, axis=-1, keepdims=True)
    )
    branch = residual.astype(BF)
    pieces_ref[:, ds : 2 * ds, :] = (
        tn(mixed_ref[...], branch).astype(BF).reshape(n_shard, ds, WIDTH)
    )
    mixed_grad = nt(branch, pack_ref[:, ds : 2 * ds, :].reshape(WIDTH, WIDTH)).astype(BF)
    for b in range(SEQUENCES):
        rows = slice(b * SLOT, (b + 1) * SLOT)
        for g in range(KV_HEADS):
            at = 2 * HEAD * g
            q2 = jnp.concatenate(
                [q_ref[rows, at : at + HEAD], q_ref[rows, at + HEAD : at + 2 * HEAD]], axis=0
            )
            out2 = jnp.concatenate(
                [mixed_grad[rows, at : at + HEAD], mixed_grad[rows, at + HEAD : at + 2 * HEAD]],
                axis=0,
            )
            keys = kv_ref[rows, HEAD * g : HEAD * (g + 1)]
            values = kv_ref[rows, FF + HEAD * g : FF + HEAD * (g + 1)]
            probs = probs_ref[b, g]
            probs_grad = nt(out2, values)
            inner = jnp.sum(probs_grad * probs, axis=-1, keepdims=True)
            scores_grad = (probs * (probs_grad - inner)).astype(BF)
            turned = nn(scores_grad, keys) * HEAD**-0.5
            dq_ref[rows, at : at + 2 * HEAD] = jnp.concatenate(
                [turned[:SLOT], turned[SLOT:]], axis=1
            )
            dkv_ref[rows, HEAD * g : HEAD * (g + 1)] = tn(scores_grad, q2) * HEAD**-0.5
            dkv_ref[rows, FF + HEAD * g : FF + HEAD * (g + 1)] = tn(probs.astype(BF), out2)
    cosine, sine = cos_ref[...], sin_ref[...]
    q_back = turn(dq_ref[...], cosine, sine, -1.0).astype(BF)
    kv_back = jnp.concatenate(
        [turn(dkv_ref[:, 0:FF], cosine, sine, -1.0).astype(BF), dkv_ref[:, FF:].astype(BF)], axis=1
    )
    normed = normed_ref[...]
    pieces_ref[:, 0:ds, :] = tn(normed, q_back).astype(BF).reshape(n_shard, ds, WIDTH)
    pieces_ref[:, 2 * ds : 3 * ds, :] = tn(normed, kv_back).astype(BF).reshape(n_shard, ds, WIDTH)
    normed_grad = nt(q_back, pack_ref[:, 0:ds, :].reshape(WIDTH, WIDTH)) + nt(
        kv_back, pack_ref[:, 2 * ds : 3 * ds, :].reshape(WIDTH, WIDTH)
    )
    r1 = lax.rsqrt(jnp.mean(x * x, axis=-1, keepdims=True) + EPS)
    gain_one = jnp.sum(normed_grad * x * r1, axis=0, keepdims=True)
    scaled = normed_grad * gain_ref[0:1, :]
    grad_ref[...] = (
        residual + r1 * scaled - x * (r1 * r1 * r1) * jnp.mean(scaled * x, axis=-1, keepdims=True)
    ).astype(BF)
    both = jnp.concatenate(
        [gain_one, gain_two, jnp.zeros((PAD - 2, WIDTH), F32)], axis=0
    ).astype(BF)
    for s in range(n_shard):
        pieces_ref[s, 3 * ds :, :] = jnp.zeros((PAD, WIDTH), BF)
        pieces_ref[s, 3 * ds :, 0:ds] = both[:, s * ds : (s + 1) * ds]


def attention_back(ds, n_shard, *args):
    return pl.pallas_call(
        functools.partial(attention_back_kernel, ds, n_shard),
        out_shape=[
            jax.ShapeDtypeStruct((ROWS, WIDTH), BF),
            jax.ShapeDtypeStruct((n_shard, 3 * ds + PAD, WIDTH), BF),
        ],
        in_specs=[VM] * 13,
        out_specs=[VM] * 2,
        scratch_shapes=[pltpu.VMEM((ROWS, WIDTH), F32), pltpu.VMEM((ROWS, WIDTH), F32)],
        compiler_params=params(56),
        cost_estimate=cost(4e9, 20 * MIB),
        name="attention_back",
    )(*args)


def weight_copies(ds, fs, order_ref, weight, up_at, down_at, sems):
    copies = []
    for k in range(weight.shape[0]):
        place = order_ref[k]
        if up_at is not None:
            rows = pl.ds(pl.multiple_of(place * ds, ds), ds)
            copies.append(
                pltpu.make_async_copy(weight.at[k, pl.ds(0, ds)], up_at.at[rows], sems.at[0, k])
            )
        rows = pl.ds(pl.multiple_of(place * fs, fs), fs)
        copies.append(
            pltpu.make_async_copy(weight.at[k, pl.ds(ds, fs)], down_at.at[rows], sems.at[1, k])
        )
    return copies


def feed_weights(ds, fs, q, per, todo, order_ref, weights, up, down, sems):
    def copies(j, slot):
        return weight_copies(
            ds, fs, order_ref, weights[j], None if up is None else up.at[slot],
            down.at[slot], sems.at[slot],
        )

    @pl.when(q == 0)
    def _():
        for copy in copies(0, 0):
            copy.start()

    for j in range(per):

        @pl.when(q == j)
        def _(j=j):
            if j + 1 < per:
                for copy in copies(j + 1, (j + 1) % 2):
                    copy.start()
            for copy in copies(j, j % 2):
                copy.wait()

        @pl.when((q == per + j) & todo)
        def _(j=j):
            for copy in copies(j, j % 2):
                copy.start()
            for copy in copies(j, j % 2):
                copy.wait()


def expert_kernel(
    ds, fs, per, n_shard, slots_ref, todo_ref, order_ref, rows_ref, cot_ref, pos_ref, wt_ref,
    posc_ref, *rest,
):
    weights = rest[:per]
    x_out, g_out, h_out, d_out, sum_out, up, down, back, total, sems, out_sem = rest[per:]
    window, passes = window_of(n_shard)
    q = pl.program_id(0)
    j, p = q % per, q // per
    slot = j % 2
    todo = todo_ref[q] > 0
    feed_weights(ds, fs, q, per, todo, order_ref, weights, up, down, sems)
    span = n_shard * window

    @pl.when(todo)
    def _():
        wanted = lax.broadcasted_iota(jnp.int32, (window, ROWS), 0).astype(F32)
        first = (p * window).astype(F32)
        for b in range(n_shard):
            at = slice(b * window, (b + 1) * window)
            chosen = (pos_ref[j, b : b + 1, :] - first == wanted).astype(F32)
            picks = chosen.astype(BF)
            x_out[0, at, :] = nn(picks, rows_ref[b]).astype(BF)
            scale = jnp.sum(chosen * wt_ref[j, b : b + 1, :], axis=1, keepdims=True)
            g_out[0, at, :] = (nn(picks, cot_ref[b]) * scale).astype(BF)
        step = 4 * window
        for lo in range(0, span, step):
            at = slice(lo, lo + step)
            both = nn(x_out[0, at, :], up[slot])
            hidden_grad = nt(g_out[0, at, :], down[slot])
            gate, upper = both[:, :FF], both[:, FF:]
            sig = jax.nn.sigmoid(gate)
            silu = gate * sig
            h_out[0, at, :] = (silu * upper).astype(BF)
            d_out[0, at, 0:FF] = (hidden_grad * upper * sig * (1.0 + gate * (1.0 - sig))).astype(BF)
            d_out[0, at, FF:] = (hidden_grad * silu).astype(BF)
            row_grad = nt(d_out[0, at, :], up[slot]).astype(BF)
            for i in range(step // window):
                back[lo // window + i, pl.ds(pl.multiple_of(j * window, 16), window), :] = row_grad[
                    i * window : (i + 1) * window
                ]

    combine(q, p, j, todo, per, n_shard, posc_ref, None, back, total)

    @pl.when(q == passes * per - 1)
    def _():
        copy = pltpu.make_async_copy(total, sum_out, out_sem)
        copy.start()
        copy.wait()


def lane_choice(values, lanes, window):
    out = values[-1]
    for i in range(len(values) - 2, -1, -1):
        out = jnp.where(lanes < (i + 1) * window, values[i], out)
    return out


def combine(q, p, j, todo, per, n_shard, posc_ref, wtc_ref, back, total):
    window, _ = window_of(n_shard)

    def spread(table, b, lanes):
        return lane_choice([table[i, :, b : b + 1] for i in range(per)], lanes, window)

    def added(b, match, weight, source):
        if weight is None:
            return nn(match.astype(BF), source)
        exact = jnp.where(match, weight, 0.0)
        high = exact.astype(BF)
        low = (exact - high.astype(F32)).astype(BF)
        return nn(high, source) + nn(low, source)

    @pl.when(q == per - 1)
    def _():
        lanes = lax.broadcasted_iota(jnp.int32, (ROWS, per * window), 1)
        place = (lanes % window).astype(F32)
        for b in range(n_shard):
            match = spread(posc_ref, b, lanes) == place
            weight = None if wtc_ref is None else spread(wtc_ref, b, lanes)
            total[b] = added(b, match, weight, back[b]).astype(BF)

    @pl.when(todo & (p > 0))
    def _():
        place = lax.broadcasted_iota(jnp.int32, (ROWS, window), 1).astype(F32)
        first = (p * window).astype(F32)
        for b in range(n_shard):
            match = posc_ref[j, :, b : b + 1] - first == place
            weight = None if wtc_ref is None else wtc_ref[j, :, b : b + 1]
            source = back[b, pl.ds(pl.multiple_of(j * window, 16), window), :]
            total[b] = (total[b].astype(F32) + added(b, match, weight, source)).astype(BF)


def expert_pass(ds, fs, per, n_shard, slots, todo, order, rows, cot, pos, wt, posc, weights):
    window, passes = window_of(n_shard)
    span = n_shard * window
    steps = passes * per

    def out_spec(width):
        return pl.BlockSpec((1, span, width), lambda q, slots, todo, order: (slots[q], 0, 0))

    shapes = [
        ((steps, span, WIDTH), BF),
        ((steps, span, WIDTH), BF),
        ((steps, span, FF), BF),
        ((steps, span, WIDTH), BF),
        ((n_shard, ROWS, WIDTH), BF),
    ]
    return pl.pallas_call(
        functools.partial(expert_kernel, ds, fs, per, n_shard),
        out_shape=[jax.ShapeDtypeStruct(s, d) for s, d in shapes],
        grid_spec=pltpu.PrefetchScalarGridSpec(
            num_scalar_prefetch=3,
            grid=(steps,),
            in_specs=[VM] * 5 + [ANY] * per,
            out_specs=[out_spec(WIDTH), out_spec(WIDTH), out_spec(FF), out_spec(WIDTH), ANY],
            scratch_shapes=[
                pltpu.VMEM((2, WIDTH, WIDTH), BF),
                pltpu.VMEM((2, FF, WIDTH), BF),
                pltpu.VMEM((n_shard, per * window, WIDTH), BF),
                pltpu.VMEM((n_shard, ROWS, WIDTH), BF),
                pltpu.SemaphoreType.DMA((2, 2, n_shard)),
                pltpu.SemaphoreType.DMA,
            ],
        ),
        compiler_params=params(60),
        cost_estimate=cost(25e9, 60 * MIB),
        name="expert_pass",
    )(slots, todo, order, rows, cot, pos, wt, posc, *weights)


def weight_grad_kernel(ds, fs, per, n_shard, j, slots_ref, todo_ref, x_ref, g_ref, h_ref, d_ref, out_ref):
    p = pl.program_id(0)

    def sums():
        upper = tn(x_ref[0], d_ref[0]).reshape(n_shard, ds, WIDTH)
        lower = tn(h_ref[0], g_ref[0]).reshape(n_shard, fs, WIDTH)
        return upper, lower

    @pl.when(p == 0)
    def _():
        upper, lower = sums()
        out_ref[:, 0:ds, :] = upper.astype(BF)
        out_ref[:, ds:, :] = lower.astype(BF)

    @pl.when((p > 0) & (todo_ref[j + per * p] > 0))
    def _():
        upper, lower = sums()
        out_ref[:, 0:ds, :] = (out_ref[:, 0:ds, :].astype(F32) + upper).astype(BF)
        out_ref[:, ds:, :] = (out_ref[:, ds:, :].astype(F32) + lower).astype(BF)


def weight_grads(ds, fs, per, n_shard, j, slots, todo, x, g, h, d):
    window, passes = window_of(n_shard)
    span = n_shard * window

    def spec(width):
        return pl.BlockSpec(
            (1, span, width),
            lambda p, slots, todo: (j + per * p * todo[j + per * p], 0, 0),
        )

    return pl.pallas_call(
        functools.partial(weight_grad_kernel, ds, fs, per, n_shard, j),
        out_shape=jax.ShapeDtypeStruct((n_shard, ds + fs, WIDTH), BF),
        grid_spec=pltpu.PrefetchScalarGridSpec(
            num_scalar_prefetch=2,
            grid=(passes,),
            in_specs=[spec(WIDTH), spec(WIDTH), spec(FF), spec(WIDTH)],
            out_specs=pl.BlockSpec(
                (n_shard, ds + fs, WIDTH), lambda p, slots, todo: (0, 0, 0)
            ),
        ),
        compiler_params=params(48),
        cost_estimate=cost(3e9, 10 * MIB),
        name="weight_grads",
    )(slots, todo, x, g, h, d)


def output_kernel(
    ds, fs, per, n_shard, slots_ref, todo_ref, order_ref, h_ref, posc_ref, wtc_ref, *rest
):
    weights = rest[:per]
    sum_out, down, back, total, sems, out_sem = rest[per:]
    window, passes = window_of(n_shard)
    q = pl.program_id(0)
    j, p = q % per, q // per
    slot = j % 2
    todo = todo_ref[q] > 0
    feed_weights(ds, fs, q, per, todo, order_ref, weights, None, down, sems)

    @pl.when(todo)
    def _():
        out = nn(h_ref[0], down[slot]).astype(BF)
        for b in range(n_shard):
            back[b, pl.ds(pl.multiple_of(j * window, 16), window), :] = out[
                b * window : (b + 1) * window
            ]

    combine(q, p, j, todo, per, n_shard, posc_ref, wtc_ref, back, total)

    @pl.when(q == passes * per - 1)
    def _():
        copy = pltpu.make_async_copy(total, sum_out, out_sem)
        copy.start()
        copy.wait()


def expert_output(ds, fs, per, n_shard, slots, todo, order, h, posc, wtc, weights):
    window, passes = window_of(n_shard)
    span = n_shard * window
    return pl.pallas_call(
        functools.partial(output_kernel, ds, fs, per, n_shard),
        out_shape=jax.ShapeDtypeStruct((n_shard, ROWS, WIDTH), BF),
        grid_spec=pltpu.PrefetchScalarGridSpec(
            num_scalar_prefetch=3,
            grid=(passes * per,),
            in_specs=[
                pl.BlockSpec((1, span, FF), lambda q, slots, todo, order: (slots[q], 0, 0)),
                VM,
                VM,
            ]
            + [ANY] * per,
            out_specs=ANY,
            scratch_shapes=[
                pltpu.VMEM((2, FF, WIDTH), BF),
                pltpu.VMEM((n_shard, per * window, WIDTH), BF),
                pltpu.VMEM((n_shard, ROWS, WIDTH), BF),
                pltpu.SemaphoreType.DMA((2, 2, n_shard)),
                pltpu.SemaphoreType.DMA,
            ],
        ),
        compiler_params=params(48),
        cost_estimate=cost(6e9, 20 * MIB),
        name="expert_output",
    )(slots, todo, order, h, posc, wtc, *weights)


def finish_kernel(ds, fs, n_shard, order_ref, *rest):
    pieces = rest[:n_shard]
    gate_ref, up_ref, down_ref = rest[n_shard:]
    for k in range(n_shard):
        place = order_ref[k]
        gate_ref[place] = pieces[k][0, 0:ds, 0:FF].astype(F32)
        up_ref[place] = pieces[k][0, 0:ds, FF:].astype(F32)
        down_ref[place] = pieces[k][0, ds:, :].astype(F32)


def finish_weight_grads(ds, fs, n_shard, order, pieces):
    return pl.pallas_call(
        functools.partial(finish_kernel, ds, fs, n_shard),
        out_shape=[
            jax.ShapeDtypeStruct((n_shard, ds, FF), F32),
            jax.ShapeDtypeStruct((n_shard, ds, FF), F32),
            jax.ShapeDtypeStruct((n_shard, fs, WIDTH), F32),
        ],
        in_specs=[SM] + [VM] * n_shard,
        out_specs=[VM] * 3,
        compiler_params=params(32),
        cost_estimate=cost(1e6, 9 * MIB),
        name="finish_weight_grads",
    )(order, *pieces)


def per_device(
    n_expert, n_shard, tokens_in, cotangent, seq_lengths, deal_perm, routes, gate_logits,
    first_gain, query_weight, key_matrix, value_matrix, output_weight, second_gain,
    gate_weight, up_weight, down_weight,
):
    e, s = lax.axis_index("expert"), lax.axis_index("shard")
    local = EXPERTS // n_expert
    per = EXPERTS // n_shard
    ds, fs = WIDTH // n_shard, FF // n_shard
    window, passes = window_of(n_shard)
    crossed = n_expert == 4 and n_shard == 8
    x = tokens_in.reshape(ROWS, WIDTH)
    cot = cotangent.reshape(ROWS, WIDTH)

    pack = jnp.concatenate(
        [
            query_weight,
            output_weight,
            jnp.concatenate([key_matrix, value_matrix], axis=1),
            jnp.zeros((PAD, WIDTH), BF),
        ],
        axis=0,
    )
    pack = lax.all_gather(pack, "shard", axis=0, tiled=False)

    packed = jnp.concatenate(
        [jnp.concatenate([gate_weight, up_weight], axis=2), down_weight], axis=1
    )
    if crossed:
        order = s ^ jnp.arange(n_shard, dtype=jnp.int32)
        owned = (e ^ jnp.arange(per, dtype=jnp.int32)) * n_shard + s
        pieces = [lax.dynamic_index_in_dim(packed, s, 0, keepdims=True)]
        for k in range(1, n_shard):
            piece = lax.dynamic_index_in_dim(packed, s ^ k, 0, keepdims=True)
            pieces.append(lax.ppermute(piece, "shard", [(i, i ^ k) for i in range(n_shard)]))
        own = jnp.concatenate(pieces, axis=0)
        weights = [own] + [
            lax.ppermute(own, "expert", [(i, i ^ j) for i in range(n_expert)])
            for j in range(1, per)
        ]
    else:
        order = jnp.arange(n_shard, dtype=jnp.int32)
        owned = jnp.arange(per, dtype=jnp.int32) * n_shard + s
        whole = lax.all_gather(packed, "expert", axis=0, tiled=True)
        whole = lax.all_to_all(
            whole.reshape(per, n_shard, ds + fs, WIDTH), "shard",
            split_axis=1, concat_axis=1, tiled=True,
        )
        weights = [whole[j] for j in range(per)]

    table = jnp.concatenate([routes.astype(F32), jax.nn.softmax(gate_logits, axis=-1)], axis=1)
    slots_meta = jnp.concatenate(
        [
            table.reshape(SEQUENCES, SLOT * 2 * TOP),
            seq_lengths.astype(F32)[:, None],
            deal_perm.astype(F32)[:, None],
        ],
        axis=1,
    )
    group = lax.all_gather(slots_meta, "expert", axis=0, tiled=True)
    mine = (e * SEQUENCES + jnp.arange(SEQUENCES)).astype(F32)
    match = (group[:, -1][None, :] == mine[:, None]).astype(F32)
    given = jnp.sum(match[:, :, None] * group[None], axis=1)
    lengths = given[:, -2].astype(jnp.int32)
    slim = jnp.stack([first_gain, second_gain]).astype(F32)
    shared = lax.all_gather(
        jnp.concatenate([given[:, :-2], slim], axis=1), "shard", axis=0, tiled=False
    )
    gains = shared[:, :, SLOT * 2 * TOP :].transpose(1, 0, 2).reshape(2, WIDTH)
    tables = shared[:, :, : SLOT * 2 * TOP].reshape(n_shard, ROWS, 2 * TOP)
    named, shares = tables[:, :, :TOP], tables[:, :, TOP:]
    hit = named[None] == owned.astype(F32)[:, None, None, None]
    wt = jnp.sum(jnp.where(hit, shares[None], 0.0), axis=-1)
    hit = jnp.any(hit, axis=-1)
    before = jnp.triu(jnp.ones((ROWS, ROWS), F32), 1).astype(BF)
    rank = lax.dot_general(
        hit.astype(BF), before, (((2,), (0,)), ((), ())), preferred_element_type=F32
    )
    pos = jnp.where(hit, rank, -1e4)
    most = jnp.max(jnp.sum(hit.astype(jnp.int32), axis=-1), axis=-1)
    todo = jnp.concatenate(
        [jnp.ones((per,), jnp.int32)]
        + [(most > window * p).astype(jnp.int32) for p in range(1, passes)]
    )
    slots = lax.cummax(jnp.where(todo > 0, jnp.arange(passes * per, dtype=jnp.int32), 0))
    posc, wtc = pos.transpose(0, 2, 1), wt.transpose(0, 2, 1)

    cosine, sine = rotation_tables()
    cots = lax.all_gather(cot, "shard", axis=0, tiled=False)
    normed, queries, kv, probs, mixed, after, routed = attention_forward(
        ds, x, pack, gains, cosine, sine, lengths
    )
    rows = lax.all_gather(routed, "shard", axis=0, tiled=False)
    xs, gs, hs, dgs, row_sums = expert_pass(
        ds, fs, per, n_shard, slots, todo, order, rows, cots, pos, wt, posc, weights
    )
    routed_grad = lax.psum_scatter(row_sums, "shard", scatter_dimension=0, tiled=False)
    grads = [
        weight_grads(ds, fs, per, n_shard, j, slots, todo, xs, gs, hs, dgs) for j in range(per)
    ]
    out_sums = expert_output(ds, fs, per, n_shard, slots, todo, order, hs, posc, wtc, weights)
    combined = lax.psum_scatter(out_sums, "shard", scatter_dimension=0, tiled=False)
    layer_out = (after + combined.astype(F32)).astype(BF).reshape(SEQUENCES, SLOT, WIDTH)

    if crossed:
        total = grads[0].astype(F32)
        for j in range(1, per):
            total = total + lax.ppermute(
                grads[j], "expert", [(i, i ^ j) for i in range(n_expert)]
            ).astype(F32)
        total = total.astype(BF)
        landed = [lax.dynamic_index_in_dim(total, s, 0, keepdims=True)]
        for k in range(1, n_shard):
            piece = lax.dynamic_index_in_dim(total, s ^ k, 0, keepdims=True)
            landed.append(lax.ppermute(piece, "shard", [(i, i ^ k) for i in range(n_shard)]))
        gate_grad, up_grad, down_grad = finish_weight_grads(ds, fs, n_shard, order, landed)
    else:
        whole = lax.all_to_all(
            jnp.stack(grads), "shard", split_axis=1, concat_axis=1, tiled=True
        ).reshape(EXPERTS, ds + fs, WIDTH)
        whole = lax.psum_scatter(whole, "expert", scatter_dimension=0, tiled=True).astype(F32)
        gate_grad, up_grad, down_grad = (
            whole[:, :ds, :FF], whole[:, :ds, FF:], whole[:, ds:, :],
        )

    input_grad, attention_grads = attention_back(
        ds, n_shard, x, cot, after, routed_grad, normed, queries, kv, probs, mixed, pack, gains,
        cosine, sine,
    )
    summed = lax.psum_scatter(attention_grads, "shard", scatter_dimension=0, tiled=False)
    summed = lax.psum(summed, "expert").astype(F32)
    return (
        layer_out,
        input_grad.reshape(SEQUENCES, SLOT, WIDTH),
        summed[3 * ds, :ds],
        summed[:ds],
        summed[2 * ds : 3 * ds, :FF],
        summed[2 * ds : 3 * ds, FF:],
        summed[ds : 2 * ds],
        summed[3 * ds + 1, :ds],
        gate_grad,
        up_grad,
        down_grad,
    )


def solution(mesh):
    both = ("expert", "shard")
    rows3, rows2, rows1 = P(both, None, None), P(both, None), P(both)
    thin, wide, third = P("shard"), P("shard", None), P("expert", "shard", None)
    return jax.shard_map(
        functools.partial(per_device, mesh.shape["expert"], mesh.shape["shard"]),
        mesh=mesh,
        in_specs=(
            rows3, rows3, rows1, rows1, rows2, rows2, thin, wide, wide, wide, wide, thin,
            third, third, third,
        ),
        out_specs=(
            rows3, rows3, thin, wide, wide, wide, wide, thin, third, third, third,
        ),
        check_vma=False,
    )
```
